32 devices in a mesh: dp: 4 (over y, x), seq: 8 (over z, core).
Axes of the slice: x: 2, y: 2, z: 4, core: 2. Of those that a mesh axis runs over, the one named last changes fastest.
Arguments:
- queries: bfloat16 [4, 1024, 512], P('dp', 'seq'), may hold values from -6 to 6
- keys: bfloat16 [4, 1024, 512], P('dp', 'seq'), may hold values from -6 to 6
- values: bfloat16 [4, 1024, 512], P('dp', 'seq'), may hold values from -6 to 6
- gates: bfloat16 [4, 1024, 512], P('dp', 'seq'), may hold values from -6 to 6
- lengths: int32 [4], P('dp'), may hold values from 256 to 1024, as said below
- rab_steps: float32 [4, 16], replicated, may hold values from -3 to 3
- out_grad: bfloat16 [4, 1024, 512], P('dp', 'seq'), may hold values from -6 to 6
Outputs:
- gated: bfloat16 [4, 1024, 512], P('dp', 'seq')
- query_grad: bfloat16 [4, 1024, 512], P('dp', 'seq')
- key_grad: bfloat16 [4, 1024, 512], P('dp', 'seq')
- value_grad: bfloat16 [4, 1024, 512], P('dp', 'seq')
- gate_grad: bfloat16 [4, 1024, 512], P('dp', 'seq')
- rab_grad: float32 [4, 16], replicated
The draws below stay inside these ranges and needn't reach their ends.
Inputs may be any that keep to these rules, and one draw needn't show every extreme that they name: Events at and after position lengths[u] of user u are padding; some user fills all 1024 slots.
All inputs are finite; a program needn't handle non-finite values.
Results may differ from the reference program's by a relative error of at most 0.0057.
Values may be sent and summed in bfloat16 or wider, within the bound.
No kernel may reach another device: no remote copies, remote signals or barrier semaphores. Data moves between devices by JAX's collectives and lax.ppermute only.
A program may use at most 64 MiB of HBM per device.

```python
import jax
import jax.numpy as jnp
from jax import lax

HEADS = 4
HEAD_DIM = 128
BUCKETS = 16
WIDTH = 512
LENGTH = 1024
USERS = 4


def draw_lengths(key, part):
    key = jax.random.fold_in(key, 7)
    first_key, second_key = jax.random.split(key)
    drawn = jax.random.randint(first_key, (USERS,), LENGTH // 4, LENGTH + 1)
    longest = jax.random.randint(second_key, (), 0, USERS)
    return jnp.where(jnp.arange(USERS) == longest, LENGTH, drawn).astype(jnp.int32)


def steps_of(own_key, dims, cuts, least, top_value):
    loudness, own = 1.0, jax.random.fold_in(own_key, 6)
    for dim, blocks in cuts:
        steps = jnp.exp(jax.random.uniform(jax.random.fold_in(own, dim), (blocks,), jnp.float32, least / len(cuts), top_value / len(cuts)))
        loudness = loudness * jnp.repeat(steps, dims[dim] // blocks).reshape([-1 if axis == dim else 1 for axis in range(len(dims))])
    return loudness


def noise(rng, shape, width, bound, shards=(), kind=jnp.bfloat16):
    factor_of = steps_of(rng, shape, shards, -0.22, 0.18) if shards else 1.0
    result = jax.random.normal(rng, shape, jnp.float32) * width * factor_of
    return jnp.minimum(jnp.maximum(result, -bound), bound).astype(kind)


def setup_inputs(seed: int = 0) -> dict:
    arg_keys = jax.random.split(jax.random.key(seed), 8)
    return {
        "queries": noise(arg_keys[0], (USERS, LENGTH, WIDTH), 1.0, 6.0, ((0, 4), (1, 8))),
        "keys": noise(arg_keys[1], (USERS, LENGTH, WIDTH), 1.0, 6.0, ((0, 4), (1, 8))),
        "values": noise(arg_keys[2], (USERS, LENGTH, WIDTH), 1.0, 6.0, ((0, 4), (1, 8))),
        "gates": noise(arg_keys[3], (USERS, LENGTH, WIDTH), 1.0, 6.0, ((0, 4), (1, 8))),
        "lengths": draw_lengths(jax.random.fold_in(arg_keys[7], 71), 0),
        "rab_steps": noise(arg_keys[5], (HEADS, BUCKETS), 0.5, 3.0, (), jnp.float32),
        "out_grad": noise(arg_keys[6], (USERS, LENGTH, WIDTH), 1.0, 6.0, ((0, 4), (1, 8))),
    }


def pair_terms(query_rows, key_rows, value_rows, dgrad_rows, query_pos, key_pos, rab_steps, valid_len):
    band_width = LENGTH // BUCKETS
    query_heads = query_rows.astype(jnp.float32).reshape(query_rows.shape[0], HEADS, HEAD_DIM)
    key_heads = key_rows.astype(jnp.float32).reshape(key_rows.shape[0], HEADS, HEAD_DIM)
    raw_score = jnp.einsum("ihd,jhd->hij", query_heads, key_heads) * (HEAD_DIM ** -0.5)
    offset = query_pos[:, None] - key_pos[None, :]
    live_mask = (offset >= 0) & (query_pos[:, None] < valid_len) & (key_pos[None, :] < valid_len)
    bias_sum = jnp.zeros(raw_score.shape, jnp.float32)
    for level in range(BUCKETS):
        ramp_mask = (offset >= level * band_width).astype(jnp.float32)
        bias_sum = bias_sum + rab_steps[:, level][:, None, None] * ramp_mask[None]
    pre_act = raw_score + bias_sum
    sigmoid_pre = jax.nn.sigmoid(pre_act)
    attn_scale = LENGTH ** -0.5
    weight = jnp.where(live_mask[None], pre_act * sigmoid_pre * attn_scale, 0.0)
    dgrad_heads = dgrad_rows.astype(jnp.float32).reshape(dgrad_rows.shape[0], HEADS, HEAD_DIM)
    value_heads = value_rows.astype(jnp.float32).reshape(value_rows.shape[0], HEADS, HEAD_DIM)
    dweight = jnp.einsum("ihd,jhd->hij", dgrad_heads, value_heads)
    dpre = jnp.where(live_mask[None], dweight * attn_scale * sigmoid_pre * (1.0 + pre_act * (1.0 - sigmoid_pre)), 0.0)
    return weight, dpre, offset


def band_sums(dpre, offset):
    band_width = LENGTH // BUCKETS
    columns = []
    for level in range(BUCKETS):
        ramp_mask = (offset >= level * band_width).astype(jnp.float32)
        columns.append(jnp.sum(dpre * ramp_mask[None], axis=(1, 2)))
    return jnp.stack(columns, axis=1)


def halved(array):
    return lax.optimization_barrier(array.astype(jnp.bfloat16)).astype(jnp.float32)


def reference(queries, keys, values, gates, lengths, rab_steps, out_grad):
    block_rows = min(512, LENGTH)
    inv_root = HEAD_DIM ** -0.5

    def one_user(packed):
        user_q, user_k, user_v, user_u, user_og, valid_len = packed
        dgrad = (user_og.astype(jnp.float32) * user_u.astype(jnp.float32)).astype(jnp.bfloat16)
        key_pos = jnp.arange(LENGTH, dtype=jnp.int32)
        key_heads = user_k.astype(jnp.float32).reshape(LENGTH, HEADS, HEAD_DIM)
        value_heads = user_v.astype(jnp.float32).reshape(LENGTH, HEADS, HEAD_DIM)

        def query_block(carry, index):
            key_acc, value_acc, rab_acc = carry
            start = (index * block_rows).astype(jnp.int32)
            query_rows = lax.dynamic_slice_in_dim(user_q, start, block_rows, 0)
            dgrad_rows = lax.dynamic_slice_in_dim(dgrad, start, block_rows, 0)
            query_pos = start + jnp.arange(block_rows, dtype=jnp.int32)
            weight, dpre, offset = pair_terms(query_rows, user_k, user_v, dgrad_rows, query_pos, key_pos, rab_steps, valid_len)
            weight_half = halved(weight)
            dpre_half = halved(dpre)
            query_heads = query_rows.astype(jnp.float32).reshape(block_rows, HEADS, HEAD_DIM)
            dgrad_heads = dgrad_rows.astype(jnp.float32).reshape(block_rows, HEADS, HEAD_DIM)
            attended = jnp.einsum("hij,jhd->ihd", weight_half, value_heads).reshape(block_rows, WIDTH)
            query_part = jnp.einsum("hij,jhd->ihd", dpre_half, key_heads).reshape(block_rows, WIDTH) * inv_root
            key_acc = key_acc + jnp.einsum("hij,ihd->jhd", dpre_half, query_heads).reshape(LENGTH, WIDTH) * inv_root
            value_acc = value_acc + jnp.einsum("hij,ihd->jhd", weight_half, dgrad_heads).reshape(LENGTH, WIDTH)
            rab_acc = rab_acc + band_sums(dpre, offset)
            return (key_acc, value_acc, rab_acc), (attended, query_part)

        start_carry = (jnp.zeros((LENGTH, WIDTH), jnp.float32), jnp.zeros((LENGTH, WIDTH), jnp.float32), jnp.zeros((HEADS, BUCKETS), jnp.float32))
        final_carry, stacked = lax.scan(query_block, start_carry, jnp.arange(LENGTH // block_rows, dtype=jnp.int32))
        key_acc, value_acc, rab_acc = final_carry
        attended = stacked[0].reshape(LENGTH, WIDTH)
        query_acc = stacked[1].reshape(LENGTH, WIDTH)
        gated = (attended * user_u.astype(jnp.float32)).astype(jnp.bfloat16)
        gate_grad = (user_og.astype(jnp.float32) * attended).astype(jnp.bfloat16)
        return gated, query_acc.astype(jnp.bfloat16), key_acc.astype(jnp.bfloat16), value_acc.astype(jnp.bfloat16), gate_grad, rab_acc

    results = lax.map(one_user, (queries, keys, values, gates, out_grad, lengths))
    rab_grad = jnp.sum(results[5], axis=0) / LENGTH
    return results[0], results[1], results[2], results[3], results[4], rab_grad
```

```python
import functools

import jax
import jax.numpy as jnp
from jax import lax
from jax.experimental import pallas as pl
from jax.experimental.pallas import tpu as pltpu
from jax.sharding import PartitionSpec as P

F32 = jnp.float32
BF16 = jnp.bfloat16
VMEM = pl.BlockSpec(memory_space=pltpu.VMEM)
SMEM = pl.BlockSpec(memory_space=pltpu.SMEM)
HBM = pl.BlockSpec(memory_space=pltpu.HBM)
ANY = pl.BlockSpec(memory_space=pl.ANY)
VMEM_LIMIT = 40 * 1024 * 1024
PREP_LIMIT = 60 * 1024 * 1024


def nt_dot(left, right):
    return lax.dot_general(left, right, (((1,), (1,)), ((), ())), preferred_element_type=F32)


def prep_kernel(
    len_ref, q_ref, k_ref, v_ref, u_ref, og_ref,
    kv_same, kv_cross, qd_same, qd_cross, far_same, far_cross, near_ref,
    buf, copied,
    *, chips,
):
    copies = [
        pltpu.make_async_copy(source.at[0], buf.at[n], copied.at[n])
        for n, source in enumerate((k_ref, v_ref, q_ref, og_ref, u_ref))
    ]
    for copy in copies:
        copy.start()
    index = lax.axis_index("seq")
    chip, core = index // 2, lax.rem(index, 2)
    rows, width = buf.shape[1:]
    wide = width // 2
    live = index * rows + lax.broadcasted_iota(jnp.int32, (rows, 1), 0) < len_ref[0]
    for copy in copies:
        copy.wait()

    def lay_out(same, cross):
        near_ref[5] = buf[3, :, cross]
        near_ref[4] = buf[4, :, cross]
        grad = buf[3].astype(F32) * buf[4].astype(F32)
        buf[3] = jnp.where(live, grad, 0.0).astype(BF16)
        for n in range(2):
            kv_same[n] = buf[n, :, same]
            kv_cross[n] = buf[n, :, cross]
            near_ref[n] = buf[n, :, cross]
            qd_same[n] = buf[n + 2, :, same]
            qd_cross[n] = buf[n + 2, :, cross]
            near_ref[n + 2] = buf[n + 2, :, cross]

    lower, upper = slice(0, wide), slice(wide, width)

    @pl.when(core == 0)
    def _():
        lay_out(lower, upper)

    @pl.when(core == 1)
    def _():
        lay_out(upper, lower)

    @pl.when(chip < chips // 2)
    def _():
        far_same[...] = kv_same[...]
        far_cross[...] = kv_cross[...]

    @pl.when(chip >= chips // 2)
    def _():
        far_same[...] = qd_same[...]
        far_cross[...] = qd_cross[...]


def prepare(lengths, queries, keys, values, gates, out_grad, chips):
    rows, width = queries.shape[1:]
    pair = jax.ShapeDtypeStruct((2, rows, width // 2), BF16)
    return pl.pallas_call(
        functools.partial(prep_kernel, chips=chips),
        out_shape=(pair,) * 6 + (jax.ShapeDtypeStruct((6, rows, width // 2), BF16),),
        in_specs=[SMEM] + [HBM] * 5,
        out_specs=(VMEM,) * 7,
        scratch_shapes=[pltpu.VMEM((5, rows, width), BF16), pltpu.SemaphoreType.DMA((5,))],
        compiler_params=pltpu.CompilerParams(vmem_limit_bytes=PREP_LIMIT),
        name="prep",
    )(lengths, queries, keys, values, gates, out_grad)


class Blocks:
    def __init__(self, cum, rab, span, depth, heads, bands, band_width, inv_root):
        self.cum, self.rab, self.span, self.depth, self.heads = cum, rab, span, depth, heads
        self.bands, self.band_width, self.inv_root = bands, band_width, inv_root
        self.rows = span // 2
        self.sub = min(self.rows, band_width)
        self.strips = self.rows // self.sub
        self.row_at = lax.broadcasted_iota(jnp.int32, (self.sub, span), 0)
        self.lane_at = lax.broadcasted_iota(jnp.int32, (self.sub, span), 1)
        self.lane_in = lax.rem(self.lane_at, self.sub)
        self.lane_strip = self.lane_at[:1, : self.rows] // self.sub

    def sum_steps(self, steps_ref, core):
        for head in range(self.heads):
            total = steps_ref[core * self.heads + head, 0]
            self.cum[head, 0] = total
            for level in range(1, self.bands):
                total = total + steps_ref[core * self.heads + head, level]
                self.cum[head, level] = total

    def level_of(self, gap, under):
        return jnp.clip(jnp.maximum(gap * self.sub - under, 0) // self.band_width, 0, self.bands - 1)

    def table(self, head, gap, sign, under):
        table = []
        for half in range(2):
            values = None
            for lane_no in range(self.strips):
                level = self.level_of(sign * (gap - half * self.strips - lane_no), under)
                value = jnp.full((1, self.rows), self.cum[head, level], F32)
                values = value if values is None else jnp.where(self.lane_strip == lane_no, value, values)
            table.append(values)
        return jnp.concatenate(table, axis=1)

    def run(self, left, right, gap, side, diagonal=False, acc=None):
        sign = 1 - 2 * side
        near = (self.row_at - self.lane_in) * sign >= 0
        for head in range(self.heads):
            cols = slice(head * self.depth, (head + 1) * self.depth)
            left_a, left_b = left(0, cols), left(1, cols)
            right_a, right_b = right(0, cols), right(1, cols)
            score = nt_dot(left_a, right_a)
            dweight = nt_dot(left_b, right_b)
            weights, dpres = [], []
            for strip in range(score.shape[0] // self.sub):
                part = slice(strip * self.sub, (strip + 1) * self.sub)
                bias = jnp.where(
                    near, self.table(head, gap + strip, sign, 0), self.table(head, gap + strip, sign, 1)
                )
                pre = score[part] * self.inv_root + bias
                bottom = 1.0 + jnp.exp2(jnp.maximum(pre, -87.0) * -1.4426950408889634)
                sig = pl.reciprocal(bottom, approx=True)
                sig = sig * (2.0 - bottom * sig)
                weight = pre * sig
                dpre = dweight[part] * (sig + weight * (1.0 - sig))
                if diagonal:
                    causal = (self.row_at + strip * self.sub - self.lane_at) * sign >= 0
                    weight = jnp.where(causal, weight, 0.0)
                    dpre = jnp.where(causal, dpre, 0.0)
                if acc is not None:
                    weights.append(weight.astype(BF16))
                    dpres.append(dpre.astype(BF16))
                whole = jnp.sum(dpre.reshape(self.sub // 8, 8, self.span), axis=0)
                inner = jnp.sum(jnp.where(near, dpre, 0.0).reshape(self.sub // 8, 8, self.span), axis=0)
                for half in range(2):
                    lanes = slice(half * self.rows, (half + 1) * self.rows)
                    for under, amount in ((0, inner[:, lanes]), (1, (whole - inner)[:, lanes])):
                        level = self.level_of(gap + strip - half * self.strips, under)
                        self.rab[head, jnp.where(side == 0, level, self.bands)] += amount
            if acc is not None:
                weight = jnp.concatenate(weights, axis=0)
                dpre = jnp.concatenate(dpres, axis=0)
                acc[side, 0, :, cols] += jnp.dot(weight, right_b, preferred_element_type=F32)
                acc[side, 1, :, cols] += jnp.dot(dpre, right_a, preferred_element_type=F32)

    def band_tile(self, out_ref, core, scale):
        lanes = lax.broadcasted_iota(jnp.int32, (self.bands, self.rows), 1) // self.sub
        level = lax.broadcasted_iota(jnp.int32, (self.bands, 128), 0)
        step_no = lax.broadcasted_iota(jnp.int32, (self.bands, 128), 1)
        out_ref[...] = jnp.zeros_like(out_ref)
        for head in range(self.heads):
            sums = jnp.sum(self.rab[head, : self.bands], axis=1)
            result = jnp.zeros((self.bands, 128), F32)
            for strip in range(self.strips):
                amount = jnp.sum(jnp.where(lanes == strip, sums, 0.0), axis=1, keepdims=True)
                result = result + jnp.where(level - strip >= step_no, amount, 0.0)
            row = jnp.sum(result, axis=0, keepdims=True) * scale
            row = jnp.broadcast_to(row, (out_ref.shape[0], 1, 128))
            for half in range(2):

                @pl.when(core == half)
                def _():
                    place = half * self.heads + head
                    out_ref[:, place : place + 1, :] = row


def position(rows):
    index = lax.axis_index("seq")
    chip, core = index // 2, lax.rem(index, 2)
    mine = pl.ds(pl.multiple_of(core * rows, rows), rows)
    others = pl.ds(pl.multiple_of((1 - core) * rows, rows), rows)
    return chip, core, mine, others


def first_kernel(
    steps_ref, kv_same, qd_same, near_ref, kv_ref, qd_ref, acc, rab, copied, cum, *, blocks_of
):
    rows = kv_same.shape[1]
    chip, core, mine, others = position(rows)
    copies = []
    for n in range(2):
        copies += [
            pltpu.make_async_copy(kv_same.at[n], kv_ref.at[n, mine], copied.at[0, n]),
            pltpu.make_async_copy(qd_same.at[n], qd_ref.at[n, mine], copied.at[1, n]),
            pltpu.make_async_copy(near_ref.at[n], kv_ref.at[n, others], copied.at[2, n]),
            pltpu.make_async_copy(near_ref.at[n + 2], qd_ref.at[n, others], copied.at[3, n]),
        ]
    for copy in copies:
        copy.start()
    acc[...] = jnp.zeros_like(acc)
    rab[...] = jnp.zeros_like(rab)
    blocks = blocks_of(cum, rab)
    blocks.sum_steps(steps_ref, core)
    for copy in copies:
        copy.wait()
    kv, qd = lambda n, cols: kv_ref[n, :, cols], lambda n, cols: qd_ref[n, :, cols]
    blocks.run(qd, kv, jnp.int32(0), 0, diagonal=True, acc=acc)
    blocks.run(kv, qd, jnp.int32(0), 1, diagonal=True, acc=acc)


def middle_kernel(*refs, ways, extra, blocks_of, scale):
    count = len(ways)
    steps_ref, kv_ref, qd_ref, acc_in, rab_in = refs[:5]
    pieces = refs[5 : 5 + 2 * count]
    acc, band_ref, stack, copied, rab, cum, plan = refs[5 + 2 * count :]
    rows = kv_ref.shape[1] // 2
    chip, core, mine, others = position(rows)
    chips = lax.axis_size("seq") // 2

    def arrivals(unit):
        return [
            pltpu.make_async_copy(pieces[2 * unit], stack.at[unit, :, mine], copied.at[0, unit]),
            pltpu.make_async_copy(pieces[2 * unit + 1], stack.at[unit, :, others], copied.at[1, unit]),
        ]

    for unit in range(count):
        for copy in arrivals(unit):
            copy.start()
    acc[...] = acc_in[...]
    rab[...] = rab_in[...]
    blocks = blocks_of(cum, rab)
    blocks.sum_steps(steps_ref, core)
    for unit, (way, hops) in enumerate(ways):
        below, above = chip >= hops, chip + hops < chips
        if way == "up":
            known, origin = below, chip - hops
        elif way == "down":
            known, origin = above, chip + hops
        else:
            known, origin = below | above, jnp.where(below, chip - hops, chip + hops)
        plan[unit] = jnp.where(known, origin, chip)
    for unit in range(count):
        for copy in arrivals(unit):
            copy.wait()
    per_chip = 2 * blocks.strips

    def step(unit, unused):
        origin = plan[unit]
        other = lambda n, cols: stack[unit, n, :, cols]
        gap = (chip - origin) * per_chip

        @pl.when(origin < chip)
        def _():
            blocks.run(lambda n, cols: qd_ref[n, :, cols], other, gap, 0, acc=acc)

        @pl.when(origin > chip)
        def _():
            blocks.run(lambda n, cols: kv_ref[n, :, cols], other, gap, 1, acc=acc)

        return unused

    lax.fori_loop(0, count, step, 0)

    up, down, far = extra
    half = chips // 2

    @pl.when((chip == half - 1) | (chip == half))
    def _():
        upper = chip - (half - 1)
        from_last = jnp.where(upper == 1, down, far)
        from_first = jnp.where(upper == 1, far, up)
        part = pl.ds(pl.multiple_of(upper * rows, rows), rows)
        blocks.run(
            lambda n, cols: stack[from_last, n, part, cols],
            lambda n, cols: stack[from_first, n, :, cols],
            (chips - 1) * per_chip + upper * blocks.strips,
            0,
        )

    blocks.band_tile(band_ref, core, scale)


def last_kernel(
    steps_ref, len_ref, kv_ref, qd_ref, acc_in, same_ref, cross_ref, near_ref, u_ref, og_ref,
    keep_ref, give_ref, stack, gate_buf, copied, acc, rab, cum,
    *, blocks_of, scale, inv_root,
):
    rows = kv_ref.shape[1] // 2
    wide = kv_ref.shape[2]
    chip, core, mine, others = position(rows)
    chips = lax.axis_size("seq") // 2
    copies = [
        pltpu.make_async_copy(same_ref, stack.at[:, mine], copied.at[0]),
        pltpu.make_async_copy(cross_ref, stack.at[:, others], copied.at[1]),
        pltpu.make_async_copy(near_ref.at[pl.ds(4, 2)], gate_buf, copied.at[2]),
    ]
    for copy in copies:
        copy.start()
    acc[...] = acc_in[...]
    blocks = blocks_of(cum, rab)
    blocks.sum_steps(steps_ref, core)
    for copy in copies:
        copy.wait()
    other = lambda n, cols: stack[n, :, cols]
    gap = (chips - 1) * 2 * blocks.strips

    @pl.when(chip == chips - 1)
    def _():
        blocks.run(lambda n, cols: qd_ref[n, :, cols], other, gap, 0, acc=acc)

    @pl.when(chip == 0)
    def _():
        blocks.run(lambda n, cols: kv_ref[n, :, cols], other, -gap, 1, acc=acc)

    def finish(out_ref, place, whose, gate, grad):
        start = (2 * chip + whose) * rows
        live = start + lax.broadcasted_iota(jnp.int32, (rows, 1), 0) < len_ref[0]
        attended = jnp.where(live, acc[0, 0, place] * scale, 0.0)
        out_ref[0] = (attended * gate.astype(F32)).astype(BF16)
        out_ref[1] = (acc[0, 1, place] * (scale * inv_root)).astype(BF16)
        out_ref[2] = (acc[1, 1, place] * (scale * inv_root)).astype(BF16)
        out_ref[3] = (acc[1, 0, place] * scale).astype(BF16)
        out_ref[4] = (attended * grad.astype(F32)).astype(BF16)

    finish(give_ref, others, 1 - core, gate_buf[0], gate_buf[1])
    for half in range(2):

        @pl.when(core == half)
        def _():
            cols = slice(half * wide, (half + 1) * wide)
            finish(keep_ref, mine, core, u_ref[0, :, cols], og_ref[0, :, cols])


def assemble_kernel(keep_ref, got_ref, *refs):
    outs, (buf, copied) = refs[:5], refs[5:]
    wide = keep_ref.shape[2]
    core = lax.rem(lax.axis_index("seq"), 2)
    for half in range(2):

        @pl.when(core == half)
        def _():
            buf[:, :, half * wide : (half + 1) * wide] = keep_ref[...]
            buf[:, :, (1 - half) * wide : (2 - half) * wide] = got_ref[...]

    copies = [pltpu.make_async_copy(buf.at[n], out.at[0], copied.at[n]) for n, out in enumerate(outs)]
    for copy in copies:
        copy.start()
    for copy in copies:
        copy.wait()


def params(units, span, wide, **more):
    return dict(
        compiler_params=pltpu.CompilerParams(vmem_limit_bytes=VMEM_LIMIT),
        cost_estimate=pl.CostEstimate(
            flops=int(units * 8 * span * span * wide * 10),
            bytes_accessed=int((units + 2) * 4 * span * wide),
            transcendentals=0,
        ),
        **more,
    )


def body(queries, keys, values, gates, lengths, rab_steps, out_grad, dp_size, seq_size):
    rows, width = queries.shape[1:]
    heads, bands = rab_steps.shape
    total_len = rows * seq_size
    chips, half = seq_size // 2, seq_size // 4
    span, wide, depth = 2 * rows, width // 2, width // heads
    inv_root, scale = depth**-0.5, total_len**-0.5
    blocks_of = functools.partial(
        Blocks, span=span, depth=depth, heads=heads // 2, bands=bands, band_width=total_len // bands, inv_root=inv_root
    )

    def send(value, hops, cross):
        pairs = [
            (2 * n + core, 2 * (n + far) + (1 - core if cross else core))
            for far, whence in hops
            for n in whence
            for core in range(2)
        ]
        return lax.ppermute(value, "seq", pairs)

    kv_same, kv_cross, qd_same, qd_cross, far_same, far_cross, near = prepare(
        lengths, queries, keys, values, gates, out_grad, chips
    )
    far_route = [(half, range(half)), (-half, range(half, chips))]
    across = [send(far_same, far_route, False), send(far_cross, far_route, True)]
    ways, pieces = [], []
    for hops in range(1, half):
        up, down = [(hops, range(chips - hops))], [(-hops, range(hops, chips))]
        ways += [("up", hops), ("down", hops)]
        pieces += [send(kv_same, up, False), send(kv_cross, up, True)]
        pieces += [send(qd_same, down, False), send(qd_cross, down, True)]
    extra = (len(ways) - 2, len(ways) - 1, len(ways))
    near = send(near, [(0, range(chips))], True)

    acc = jax.ShapeDtypeStruct((2, 2, span, wide), F32)
    rab = jax.ShapeDtypeStruct((heads // 2, bands + 1, 8, rows), F32)
    own = jax.ShapeDtypeStruct((2, span, wide), BF16)
    cum = pltpu.SMEM((heads // 2, bands), F32)
    own_kv, own_qd, acc_now, rab_now = pl.pallas_call(
        functools.partial(first_kernel, blocks_of=blocks_of),
        out_shape=(own, own, acc, rab),
        in_specs=[SMEM, ANY, ANY, ANY],
        out_specs=(VMEM,) * 4,
        scratch_shapes=[pltpu.SemaphoreType.DMA((4, 2)), cum],
        **params(2, span, wide, name="attend_own"),
    )(rab_steps, kv_same, qd_same, near)

    acc_now, across = lax.optimization_barrier((acc_now, across))
    for hops in range(half, chips - 1):
        ways.append(("either", hops))
        pieces += across
        onward = [(1, range(hops, chips - 1)), (-1, range(1, chips - hops))]
        across = [send(value, onward, False) for value in across]
    count = dp_size * seq_size
    together = count <= 64
    acc_now, band = pl.pallas_call(
        functools.partial(middle_kernel, ways=tuple(ways), extra=extra, blocks_of=blocks_of, scale=scale),
        out_shape=(acc, jax.ShapeDtypeStruct((count if together else seq_size, 8, 128), F32)),
        in_specs=[SMEM] + [VMEM] * 4 + [ANY] * len(pieces),
        out_specs=(VMEM,) * 2,
        scratch_shapes=[
            pltpu.VMEM((len(ways), 2, span, wide), BF16),
            pltpu.SemaphoreType.DMA((2, len(ways))),
            pltpu.VMEM(rab.shape, F32),
            cum,
            pltpu.SMEM((len(ways),), jnp.int32),
        ],
        **params(len(ways), span, wide, name="attend_middle"),
    )(rab_steps, own_kv, own_qd, acc_now, rab_now, *pieces)
    band = lax.all_to_all(band, ("dp", "seq") if together else "seq", 0, 0)

    band, across = lax.optimization_barrier((band, across))
    half_out = jax.ShapeDtypeStruct((5, rows, wide), BF16)
    keep, give = pl.pallas_call(
        functools.partial(last_kernel, blocks_of=blocks_of, scale=scale, inv_root=inv_root),
        out_shape=(half_out, half_out),
        in_specs=[SMEM, SMEM] + [VMEM] * 3 + [ANY] * 3 + [VMEM] * 2,
        out_specs=(VMEM,) * 2,
        scratch_shapes=[
            pltpu.VMEM((2, span, wide), BF16),
            pltpu.VMEM((2, rows, wide), BF16),
            pltpu.SemaphoreType.DMA((3,)),
            pltpu.VMEM(acc.shape, F32),
            pltpu.VMEM(rab.shape, F32),
            cum,
        ],
        **params(1, span, wide, name="attend_last"),
    )(rab_steps, lengths, own_kv, own_qd, acc_now, *across, near, gates, out_grad)
    got = send(give, [(0, range(chips))], True)
    out = jax.ShapeDtypeStruct(queries.shape, BF16)
    outs = pl.pallas_call(
        assemble_kernel,
        out_shape=(out,) * 5,
        in_specs=[VMEM, VMEM],
        out_specs=(HBM,) * 5,
        scratch_shapes=[pltpu.VMEM((5, rows, width), BF16), pltpu.SemaphoreType.DMA((5,))],
        compiler_params=pltpu.CompilerParams(vmem_limit_bytes=VMEM_LIMIT),
        name="assemble",
    )(keep, got)
    band = jnp.sum(band, axis=0)
    if not together:
        band = lax.psum(band, "dp")
    return (*outs, band[:heads, :bands] / total_len)


def solution(mesh):
    rows = P("dp", "seq", None)
    return jax.shard_map(
        functools.partial(body, dp_size=mesh.shape["dp"], seq_size=mesh.shape["seq"]),
        mesh=mesh,
        in_specs=(rows, rows, rows, rows, P("dp"), P(), rows),
        out_specs=(rows, rows, rows, rows, rows, P()),
        check_vma=False,
    )
```

```python
import functools

import jax
import jax.numpy as jnp
from jax import lax
from jax.experimental import pallas as pl
from jax.experimental.pallas import tpu as pltpu
from jax.sharding import PartitionSpec as P

F32 = jnp.float32
BF16 = jnp.bfloat16
VMEM = pl.BlockSpec(memory_space=pltpu.VMEM)
SMEM = pl.BlockSpec(memory_space=pltpu.SMEM)
HBM = pl.BlockSpec(memory_space=pltpu.HBM)
ANY = pl.BlockSpec(memory_space=pl.ANY)
VMEM_LIMIT = 40 * 1024 * 1024
PREP_LIMIT = 60 * 1024 * 1024


def nt_dot(left, right):
    return lax.dot_general(left, right, (((1,), (1,)), ((), ())), preferred_element_type=F32)


class Round:
    def __init__(self, chips, payload, route, earlier=()):
        self.payload, self.route = payload, route
        self.origin = list(range(chips))
        for source, target in route.items():
            self.origin[target] = source if isinstance(payload, str) else earlier[payload].origin[source]


def plan_rounds(chips):
    half = chips // 2
    early, late = [], []

    def add(rounds, payload, route):
        rounds.append(Round(chips, payload, route, early))
        return len(rounds) - 1

    if chips == 4:
        across = add(early, "even", {0: 2, 3: 1, 1: 0, 2: 3})
        inner = add(early, "low", {1: 2, 2: 1})
        outer = add(early, "low", {0: 1, 3: 2})
        add(late, across, {2: 3, 1: 0})
        add(late, inner, {2: 3, 1: 0})
        return early, late, {across: (1,)}, {1: (across, outer, 0), 2: (outer, across, 1)}
    far = add(early, "low", {n: n + half if n < half else n - half for n in range(chips)})
    for hops in range(1, half):
        up = add(early, "kv", {n: n + hops for n in range(chips - hops)})
        down = add(early, "qd", {n: n - hops for n in range(hops, chips)})
    held = far
    for hops in range(half, chips - 1):
        route = {n: n + 1 for n in range(hops, chips - 1)} | {n: n - 1 for n in range(1, chips - hops)}
        held = add(early if hops < chips - 2 else late, held, route)
    return early, late, {}, {half - 1: (far, up, 0), half: (down, far, 1)}


def of_chip(table, chip):
    result = jnp.int32(table[0])
    for n in range(1, len(table)):
        result = jnp.where(chip == n, jnp.int32(table[n]), result)
    return result


def prep_kernel(len_ref, k_ref, v_ref, q_ref, u_ref, og_ref, same_ref, cross_ref, buf, copied):
    copies = [
        pltpu.make_async_copy(source.at[0], buf.at[n], copied.at[n])
        for n, source in enumerate((k_ref, v_ref, q_ref, u_ref, og_ref))
    ]
    for copy in copies:
        copy.start()
    rows, width = buf.shape[1:]
    wide = width // 2
    index = lax.axis_index("seq")
    live = index * rows + lax.broadcasted_iota(jnp.int32, (rows, 1), 0) < len_ref[0]
    for copy in copies:
        copy.wait()
    for half in range(2):
        cols = slice(half * wide, (half + 1) * wide)
        grad = buf[3, :, cols].astype(F32) * buf[4, :, cols].astype(F32)
        grad = jnp.where(live, grad, 0.0).astype(BF16)

        def lay_out(out_ref):
            for n in range(3):
                out_ref[n] = buf[n, :, cols]
            out_ref[3] = grad
            out_ref[4] = buf[3, :, cols]
            out_ref[5] = buf[4, :, cols]

        @pl.when(lax.rem(index, 2) == half)
        def _():
            lay_out(same_ref)

        @pl.when(lax.rem(index, 2) != half)
        def _():
            lay_out(cross_ref)


def build_kernel(same_ref, near_ref, kv_ref, qd_ref, gate_ref, low_ref, even_ref, *, chips):
    chip, _, mine, others = position(same_ref.shape[1])
    for place, source in ((mine, same_ref), (others, near_ref)):
        for n, out_ref in enumerate((kv_ref, qd_ref, gate_ref)):
            out_ref[0, place] = source[2 * n]
            out_ref[1, place] = source[2 * n + 1]

    for out_ref, keys_go in ((low_ref, chip < chips // 2), (even_ref, lax.rem(chip, 2) == 0)):

        @pl.when(keys_go)
        def _():
            out_ref[...] = kv_ref[...]

        @pl.when(jnp.logical_not(keys_go))
        def _():
            out_ref[...] = qd_ref[...]


class Blocks:
    def __init__(self, cum, rab, span, depth, heads, bands, band_width, inv_root):
        self.cum, self.rab, self.span, self.depth, self.heads = cum, rab, span, depth, heads
        self.bands, self.band_width, self.inv_root = bands, band_width, inv_root
        self.rows = span // 2
        self.sub = min(self.rows, band_width)
        self.strips = self.rows // self.sub
        self.row_at = lax.broadcasted_iota(jnp.int32, (self.sub, span), 0)
        self.lane_at = lax.broadcasted_iota(jnp.int32, (self.sub, span), 1)
        self.lane_in = lax.rem(self.lane_at, self.sub)
        self.lane_strip = self.lane_at[:1, : self.rows] // self.sub

    def sum_steps(self, steps_ref, core):
        for head in range(self.heads):
            total = steps_ref[core * self.heads + head, 0]
            self.cum[head, 0] = total
            for level in range(1, self.bands):
                total = total + steps_ref[core * self.heads + head, level]
                self.cum[head, level] = total

    def level_of(self, gap, under):
        return jnp.clip(jnp.maximum(gap * self.sub - under, 0) // self.band_width, 0, self.bands - 1)

    def table(self, head, gap, sign, under):
        table = []
        for half in range(2):
            values = None
            for lane_no in range(self.strips):
                level = self.level_of(sign * (gap - half * self.strips - lane_no), under)
                value = jnp.full((1, self.rows), self.cum[head, level], F32)
                values = value if values is None else jnp.where(self.lane_strip == lane_no, value, values)
            table.append(values)
        return jnp.concatenate(table, axis=1)

    def run(self, left, right, gap, side, diagonal=False, acc=None, banded=None):
        sign = 1 - 2 * side
        near = (self.row_at - self.lane_in) * sign >= 0
        for head in range(self.heads):
            cols = slice(head * self.depth, (head + 1) * self.depth)
            left_a, left_b = left(0, cols), left(1, cols)
            right_a, right_b = right(0, cols), right(1, cols)
            score = nt_dot(left_a, right_a)
            dweight = nt_dot(left_b, right_b)
            weights, dpres = [], []
            for strip in range(score.shape[0] // self.sub):
                part = slice(strip * self.sub, (strip + 1) * self.sub)
                bias = jnp.where(
                    near, self.table(head, gap + strip, sign, 0), self.table(head, gap + strip, sign, 1)
                )
                pre = score[part] * self.inv_root + bias
                bottom = 1.0 + jnp.exp2(jnp.maximum(pre, -87.0) * -1.4426950408889634)
                sig = pl.reciprocal(bottom, approx=True)
                sig = sig * (2.0 - bottom * sig)
                weight = pre * sig
                dpre = dweight[part] * (sig + weight * (1.0 - sig))
                if diagonal:
                    causal = (self.row_at + strip * self.sub - self.lane_at) * sign >= 0
                    weight = jnp.where(causal, weight, 0.0)
                    dpre = jnp.where(causal, dpre, 0.0)
                if acc is not None:
                    weights.append(weight.astype(BF16))
                    dpres.append(dpre.astype(BF16))
                if banded is None:
                    continue
                whole = jnp.sum(dpre.reshape(self.sub // 8, 8, self.span), axis=0)
                inner = jnp.sum(jnp.where(near, dpre, 0.0).reshape(self.sub // 8, 8, self.span), axis=0)
                for half in range(2):
                    lanes = slice(half * self.rows, (half + 1) * self.rows)
                    for under, amount in ((0, inner[:, lanes]), (1, (whole - inner)[:, lanes])):
                        level = self.level_of(sign * (gap + strip - half * self.strips), under)
                        self.rab[side, head, jnp.where(banded, level, self.bands)] += amount
            if acc is not None:
                weight = jnp.concatenate(weights, axis=0)
                dpre = jnp.concatenate(dpres, axis=0)
                acc[side, 0, :, cols] += jnp.dot(weight, right_b, preferred_element_type=F32)
                acc[side, 1, :, cols] += jnp.dot(dpre, right_a, preferred_element_type=F32)

    def band_row(self, out_ref, core, scale):
        strip_of = lax.broadcasted_iota(jnp.int32, (self.bands, self.rows), 1) // self.sub
        level = lax.broadcasted_iota(jnp.int32, (self.bands, 128), 0)
        lane = lax.broadcasted_iota(jnp.int32, (self.bands, 128), 1)
        result = jnp.zeros((self.bands, 128), F32)
        for head in range(self.heads):
            step_no = lane - (core * self.heads + head) * self.bands
            inside = (step_no >= 0) & (step_no < self.bands)
            for side in range(2):
                sums = jnp.sum(self.rab[side, head, : self.bands], axis=1)
                for strip in range(self.strips):
                    amount = jnp.sum(jnp.where(strip_of == strip, sums, 0.0), axis=1, keepdims=True)
                    band = level - strip if side == 0 else level + strip
                    result = result + jnp.where(inside & (band >= step_no), amount, 0.0)
        out_ref[...] = jnp.sum(result, axis=0, keepdims=True) * scale


def position(rows):
    index = lax.axis_index("seq")
    chip, core = index // 2, lax.rem(index, 2)
    mine = pl.ds(pl.multiple_of(core * rows, rows), rows)
    others = pl.ds(pl.multiple_of((1 - core) * rows, rows), rows)
    return chip, core, mine, others


def own_kernel(steps_ref, kv_ref, qd_ref, acc, rab, cum, *, blocks_of):
    chip, core, _, _ = position(kv_ref.shape[1] // 2)
    acc[...] = jnp.zeros_like(acc)
    rab[...] = jnp.zeros_like(rab)
    blocks = blocks_of(cum, rab)
    blocks.sum_steps(steps_ref, core)
    kv, qd = lambda n, cols: kv_ref[n, :, cols], lambda n, cols: qd_ref[n, :, cols]
    blocks.run(qd, kv, jnp.int32(0), 0, diagonal=True, acc=acc, banded=True)
    blocks.run(kv, qd, jnp.int32(0), 1, diagonal=True, acc=acc)


def middle_kernel(*refs, rounds, key_side, ends, blocks_of, scale):
    count = len(rounds)
    steps_ref, kv_ref, qd_ref, acc_in, rab_in = refs[:5]
    pieces = refs[5 : 5 + count]
    acc, band_ref, stack, copied, rab, cum, plan = refs[5 + count :]
    rows = kv_ref.shape[1] // 2
    chip, core, _, _ = position(rows)
    chips = lax.axis_size("seq") // 2
    copies = [
        pltpu.make_async_copy(piece, stack.at[unit], copied.at[unit]) for unit, piece in enumerate(pieces)
    ]
    for copy in copies:
        copy.start()
    acc[...] = acc_in[...]
    rab[...] = rab_in[...]
    blocks = blocks_of(cum, rab)
    blocks.sum_steps(steps_ref, core)
    for unit, one in enumerate(rounds):
        plan[unit, 0] = of_chip(one.origin, chip)
        plan[unit, 1] = of_chip([int(n in key_side.get(unit, ())) for n in range(chips)], chip)
    for copy in copies:
        copy.wait()
    per_chip = 2 * blocks.strips

    def step(unit, unused):
        origin = plan[unit, 0]
        other = lambda n, cols: stack[unit, n, :, cols]
        gap = (chip - origin) * per_chip

        @pl.when(origin < chip)
        def _():
            blocks.run(lambda n, cols: qd_ref[n, :, cols], other, gap, 0, acc=acc, banded=True)

        @pl.when(origin > chip)
        def _():
            wanted = plan[unit, 1] == 1
            blocks.run(lambda n, cols: kv_ref[n, :, cols], other, gap, 1, acc=acc, banded=wanted)

        return unused

    lax.fori_loop(0, count, step, 0)

    tables = [[ends.get(n, (0, 0, -1))[part] for n in range(chips)] for part in range(3)]
    queries_at, keys_at, part = [of_chip(table, chip) for table in tables]

    @pl.when(part >= 0)
    def _():
        place = pl.ds(pl.multiple_of(part * rows, rows), rows)
        blocks.run(
            lambda n, cols: stack[queries_at, n, place, cols],
            lambda n, cols: stack[keys_at, n, :, cols],
            (chips - 1) * per_chip + part * blocks.strips,
            0,
            banded=True,
        )

    blocks.band_row(band_ref, core, scale)


def last_kernel(
    steps_ref, len_ref, kv_ref, qd_ref, acc_in, gate_ref, *refs, rounds, blocks_of, scale, inv_root
):
    pieces, (keep_ref, give_ref, acc, rab, cum) = refs[: len(rounds)], refs[len(rounds) :]
    rows = kv_ref.shape[1] // 2
    chip, core, mine, others = position(rows)
    acc[...] = acc_in[...]
    blocks = blocks_of(cum, rab)
    blocks.sum_steps(steps_ref, core)
    for one, piece in zip(rounds, pieces):
        origin = of_chip(one.origin, chip)
        gap = (chip - origin) * 2 * blocks.strips
        other = lambda n, cols: piece[n, :, cols]

        @pl.when(origin < chip)
        def _():
            blocks.run(lambda n, cols: qd_ref[n, :, cols], other, gap, 0, acc=acc)

        @pl.when(origin > chip)
        def _():
            blocks.run(lambda n, cols: kv_ref[n, :, cols], other, gap, 1, acc=acc)

    for out_ref, place, whose in ((give_ref, others, 1 - core), (keep_ref, mine, core)):
        start = (2 * chip + whose) * rows
        live = start + lax.broadcasted_iota(jnp.int32, (rows, 1), 0) < len_ref[0]
        attended = jnp.where(live, acc[0, 0, place] * scale, 0.0)
        out_ref[0] = (attended * gate_ref[0, place].astype(F32)).astype(BF16)
        out_ref[1] = (acc[0, 1, place] * (scale * inv_root)).astype(BF16)
        out_ref[2] = (acc[1, 1, place] * (scale * inv_root)).astype(BF16)
        out_ref[3] = (acc[1, 0, place] * scale).astype(BF16)
        out_ref[4] = (attended * gate_ref[1, place].astype(F32)).astype(BF16)


def assemble_kernel(keep_ref, got_ref, *refs):
    outs, (buf, copied) = refs[:5], refs[5:]
    wide = keep_ref.shape[2]
    core = lax.rem(lax.axis_index("seq"), 2)
    for half in range(2):

        @pl.when(core == half)
        def _():
            buf[:, :, half * wide : (half + 1) * wide] = keep_ref[...]
            buf[:, :, (1 - half) * wide : (2 - half) * wide] = got_ref[...]

    copies = [pltpu.make_async_copy(buf.at[n], out.at[0], copied.at[n]) for n, out in enumerate(outs)]
    for copy in copies:
        copy.start()
    for copy in copies:
        copy.wait()


def rab_kernel(row_ref, rab_ref, *, total_len):
    heads, bands = rab_ref.shape
    row = row_ref[...] / total_len
    for head in range(heads):
        rab_ref[head : head + 1, :] = row[:, head * bands : (head + 1) * bands]


def sum_over(value, axis, size, flip=1):
    while flip < size:
        value = value + lax.ppermute(value, axis, [(n, n ^ flip) for n in range(size)])
        flip *= 2
    return value


def params(units, span, wide, **more):
    return dict(
        compiler_params=pltpu.CompilerParams(vmem_limit_bytes=VMEM_LIMIT),
        cost_estimate=pl.CostEstimate(
            flops=int(units * 8 * span * span * wide * 10),
            bytes_accessed=int((units + 2) * 4 * span * wide),
            transcendentals=0,
        ),
        **more,
    )


def body(queries, keys, values, gates, lengths, rab_steps, out_grad, dp_size, seq_size):
    rows, width = queries.shape[1:]
    heads, bands = rab_steps.shape
    total_len = rows * seq_size
    chips = seq_size // 2
    span, wide, depth = 2 * rows, width // 2, width // heads
    inv_root, scale = depth**-0.5, total_len**-0.5
    blocks_of = functools.partial(
        Blocks, span=span, depth=depth, heads=heads // 2, bands=bands, band_width=total_len // bands, inv_root=inv_root
    )

    def send(value, route):
        pairs = [(2 * n + core, 2 * target + core) for n, target in route.items() for core in range(2)]
        return lax.ppermute(value, "seq", pairs)

    across_chip = [(n, n ^ 1) for n in range(seq_size)]
    packed = jax.ShapeDtypeStruct((6, rows, wide), BF16)
    same, cross = pl.pallas_call(
        prep_kernel,
        out_shape=(packed, packed),
        in_specs=[SMEM] + [HBM] * 5,
        out_specs=(VMEM,) * 2,
        scratch_shapes=[pltpu.VMEM((5, rows, width), BF16), pltpu.SemaphoreType.DMA((5,))],
        compiler_params=pltpu.CompilerParams(vmem_limit_bytes=PREP_LIMIT),
        name="prep",
    )(lengths, keys, values, queries, gates, out_grad)
    own = jax.ShapeDtypeStruct((2, span, wide), BF16)
    own_kv, own_qd, gate, low, even = pl.pallas_call(
        functools.partial(build_kernel, chips=chips),
        out_shape=(own,) * 5,
        in_specs=[VMEM] * 2,
        out_specs=(VMEM,) * 5,
        compiler_params=pltpu.CompilerParams(vmem_limit_bytes=VMEM_LIMIT),
        name="build",
    )(same, lax.ppermute(cross, "seq", across_chip))

    early, late, key_side, ends = plan_rounds(chips)
    ready = {"kv": own_kv, "qd": own_qd, "low": low, "even": even}
    got = [send(ready[one.payload], one.route) if isinstance(one.payload, str) else None for one in early]

    acc = jax.ShapeDtypeStruct((2, 2, span, wide), F32)
    rab = jax.ShapeDtypeStruct((2, heads // 2, bands + 1, 8, rows), F32)
    cum = pltpu.SMEM((heads // 2, bands), F32)
    acc_now, rab_now = pl.pallas_call(
        functools.partial(own_kernel, blocks_of=blocks_of),
        out_shape=(acc, rab),
        in_specs=[SMEM, VMEM, VMEM],
        out_specs=(VMEM,) * 2,
        scratch_shapes=[cum],
        **params(2, span, wide, name="attend_own"),
    )(rab_steps, own_kv, own_qd)

    acc_now, got[0] = lax.optimization_barrier((acc_now, got[0]))
    for n, one in enumerate(early):
        if got[n] is None:
            got[n] = send(got[one.payload], one.route)
    ahead = send(got[late[0].payload], late[0].route)
    acc_now, row = pl.pallas_call(
        functools.partial(
            middle_kernel, rounds=early, key_side=key_side, ends=ends, blocks_of=blocks_of, scale=scale
        ),
        out_shape=(acc, jax.ShapeDtypeStruct((1, 128), F32)),
        in_specs=[SMEM] + [VMEM] * 4 + [ANY] * len(got),
        out_specs=(VMEM,) * 2,
        scratch_shapes=[
            pltpu.VMEM((len(early), 2, span, wide), BF16),
            pltpu.SemaphoreType.DMA((len(early),)),
            pltpu.VMEM(rab.shape, F32),
            cum,
            pltpu.SMEM((len(early), 2), jnp.int32),
        ],
        **params(len(early), span, wide, name="attend_middle"),
    )(rab_steps, own_kv, own_qd, acc_now, rab_now, *got)

    acc_now, ahead, *kept = lax.optimization_barrier((acc_now, ahead, *[got[one.payload] for one in late[1:]]))
    tail = [ahead] + [send(value, one.route) for value, one in zip(kept, late[1:])]
    row = row + lax.ppermute(row, "seq", across_chip)
    row = sum_over(row, "dp", dp_size)
    row, tail = lax.optimization_barrier((row, tail))
    row = row + lax.ppermute(row, "seq", [(n, n ^ 2) for n in range(seq_size)])
    half_out = jax.ShapeDtypeStruct((5, rows, wide), BF16)
    keep, give = pl.pallas_call(
        functools.partial(last_kernel, rounds=late, blocks_of=blocks_of, scale=scale, inv_root=inv_root),
        out_shape=(half_out, half_out),
        in_specs=[SMEM, SMEM] + [VMEM] * (4 + len(tail)),
        out_specs=(VMEM,) * 2,
        scratch_shapes=[pltpu.VMEM(acc.shape, F32), pltpu.VMEM(rab.shape, F32), cum],
        **params(len(late), span, wide, name="attend_last"),
    )(rab_steps, lengths, own_kv, own_qd, acc_now, gate, *tail)
    row, give = lax.optimization_barrier((row, give))
    row = sum_over(row, "seq", seq_size, 4)
    theirs = lax.ppermute(give, "seq", across_chip)
    out = jax.ShapeDtypeStruct(queries.shape, BF16)
    outs = pl.pallas_call(
        assemble_kernel,
        out_shape=(out,) * 5,
        in_specs=[VMEM] * 2,
        out_specs=(HBM,) * 5,
        scratch_shapes=[pltpu.VMEM((5, rows, width), BF16), pltpu.SemaphoreType.DMA((5,))],
        compiler_params=pltpu.CompilerParams(vmem_limit_bytes=VMEM_LIMIT),
        name="assemble",
    )(keep, theirs)
    rab_grad = pl.pallas_call(
        functools.partial(rab_kernel, total_len=total_len),
        out_shape=jax.ShapeDtypeStruct((heads, bands), F32),
        in_specs=[VMEM],
        out_specs=VMEM,
        name="bias_grad",
    )(row)
    return (*outs, rab_grad)


def solution(mesh):
    rows = P("dp", "seq", None)
    return jax.shard_map(
        functools.partial(body, dp_size=mesh.shape["dp"], seq_size=mesh.shape["seq"]),
        mesh=mesh,
        in_specs=(rows, rows, rows, rows, P("dp"), P(), rows),
        out_specs=(rows, rows, rows, rows, rows, P()),
        check_vma=False,
    )
```

```python
import functools

import jax
import jax.numpy as jnp
from jax import lax
from jax.experimental import pallas as pl
from jax.experimental.pallas import tpu as pltpu
from jax.sharding import PartitionSpec as P

F32 = jnp.float32
BF16 = jnp.bfloat16
VMEM = pl.BlockSpec(memory_space=pltpu.VMEM)
SMEM = pl.BlockSpec(memory_space=pltpu.SMEM)
HBM = pl.BlockSpec(memory_space=pltpu.HBM)
ANY = pl.BlockSpec(memory_space=pl.ANY)
VMEM_LIMIT = 40 * 1024 * 1024
PREP_LIMIT = 60 * 1024 * 1024


def nt_dot(left, right):
    return lax.dot_general(left, right, (((1,), (1,)), ((), ())), preferred_element_type=F32)


class Round:
    def __init__(self, chips, payload, route, earlier=()):
        self.payload, self.route = payload, route
        self.origin = list(range(chips))
        for source, target in route.items():
            self.origin[target] = source if isinstance(payload, str) else earlier[payload].origin[source]


def plan_rounds(chips):
    half = chips // 2
    early, late = [], []

    def add(rounds, payload, route):
        rounds.append(Round(chips, payload, route, early))
        return len(rounds) - 1

    if chips == 4:
        across = add(early, "even", {0: 2, 3: 1, 1: 0, 2: 3})
        inner = add(early, "low", {1: 2, 2: 1})
        outer = add(early, "low", {0: 1, 3: 2})
        add(late, across, {2: 3, 1: 0})
        add(late, inner, {2: 3, 1: 0})
        return early, late, {across: (1,)}, {1: (across, outer, 0), 2: (outer, across, 1)}
    far = add(early, "low", {n: n + half if n < half else n - half for n in range(chips)})
    for hops in range(1, half):
        up = add(early, "kv", {n: n + hops for n in range(chips - hops)})
        down = add(early, "qd", {n: n - hops for n in range(hops, chips)})
    held = far
    for hops in range(half, chips - 1):
        route = {n: n + 1 for n in range(hops, chips - 1)} | {n: n - 1 for n in range(1, chips - hops)}
        held = add(early if hops < chips - 2 else late, held, route)
    return early, late, {}, {half - 1: (far, up, 0), half: (down, far, 1)}


def of_chip(table, chip):
    result = jnp.int32(table[0])
    for n in range(1, len(table)):
        result = jnp.where(chip == n, jnp.int32(table[n]), result)
    return result


def prep_kernel(len_ref, k_ref, v_ref, q_ref, u_ref, og_ref, same_ref, cross_ref, buf, copied):
    copies = [
        pltpu.make_async_copy(source.at[0], buf.at[n], copied.at[n])
        for n, source in enumerate((k_ref, v_ref, q_ref, u_ref, og_ref))
    ]
    for copy in copies:
        copy.start()
    rows, width = buf.shape[1:]
    wide = width // 2
    index = lax.axis_index("seq")
    live = index * rows + lax.broadcasted_iota(jnp.int32, (rows, 1), 0) < len_ref[0]
    for copy in copies:
        copy.wait()
    for half in range(2):
        cols = slice(half * wide, (half + 1) * wide)
        grad = buf[3, :, cols].astype(F32) * buf[4, :, cols].astype(F32)
        grad = jnp.where(live, grad, 0.0).astype(BF16)

        def lay_out(out_ref):
            for n in range(3):
                out_ref[n] = buf[n, :, cols]
            out_ref[3] = grad
            out_ref[4] = buf[3, :, cols]
            out_ref[5] = buf[4, :, cols]

        @pl.when(lax.rem(index, 2) == half)
        def _():
            lay_out(same_ref)

        @pl.when(lax.rem(index, 2) != half)
        def _():
            lay_out(cross_ref)


def build_kernel(same_ref, near_ref, kv_ref, qd_ref, gate_ref, low_ref, even_ref, *, chips):
    chip, _, mine, others = position(same_ref.shape[1])
    for place, source in ((mine, same_ref), (others, near_ref)):
        for n, out_ref in enumerate((kv_ref, qd_ref, gate_ref)):
            out_ref[0, place] = source[2 * n]
            out_ref[1, place] = source[2 * n + 1]

    for out_ref, keys_go in ((low_ref, chip < chips // 2), (even_ref, lax.rem(chip, 2) == 0)):

        @pl.when(keys_go)
        def _():
            out_ref[...] = kv_ref[...]

        @pl.when(jnp.logical_not(keys_go))
        def _():
            out_ref[...] = qd_ref[...]


class Blocks:
    def __init__(self, cum, rab, span, depth, heads, bands, band_width, inv_root):
        self.cum, self.rab, self.span, self.depth, self.heads = cum, rab, span, depth, heads
        self.bands, self.band_width, self.inv_root = bands, band_width, inv_root
        self.rows = span // 2
        self.sub = min(self.rows, band_width)
        self.strips = self.rows // self.sub
        self.row_at = lax.broadcasted_iota(jnp.int32, (self.sub, span), 0)
        self.lane_at = lax.broadcasted_iota(jnp.int32, (self.sub, span), 1)
        self.lane_in = lax.rem(self.lane_at, self.sub)
        self.lane_strip = self.lane_at[:1, : self.rows] // self.sub

    def sum_steps(self, steps_ref, core):
        for head in range(self.heads):
            total = steps_ref[core * self.heads + head, 0]
            self.cum[head, 0] = total
            for level in range(1, self.bands):
                total = total + steps_ref[core * self.heads + head, level]
                self.cum[head, level] = total

    def level_of(self, gap, under):
        return jnp.clip(jnp.maximum(gap * self.sub - under, 0) // self.band_width, 0, self.bands - 1)

    def table(self, head, gap, sign, under):
        table = []
        for half in range(2):
            values = None
            for lane_no in range(self.strips):
                level = self.level_of(sign * (gap - half * self.strips - lane_no), under)
                value = jnp.full((1, self.rows), self.cum[head, level], F32)
                values = value if values is None else jnp.where(self.lane_strip == lane_no, value, values)
            table.append(values)
        return jnp.concatenate(table, axis=1)

    def run(self, left, right, gap, side, diagonal=False, acc=None, banded=None):
        sign = 1 - 2 * side
        near = (self.row_at - self.lane_in) * sign >= 0
        for head in range(self.heads):
            cols = slice(head * self.depth, (head + 1) * self.depth)
            left_a, left_b = left(0, cols), left(1, cols)
            right_a, right_b = right(0, cols), right(1, cols)
            score = nt_dot(left_a, right_a)
            dweight = nt_dot(left_b, right_b)
            weights, dpres = [], []
            for strip in range(score.shape[0] // self.sub):
                part = slice(strip * self.sub, (strip + 1) * self.sub)
                bias = jnp.where(
                    near, self.table(head, gap + strip, sign, 0), self.table(head, gap + strip, sign, 1)
                )
                pre = score[part] * self.inv_root + bias
                bottom = 1.0 + jnp.exp2(jnp.maximum(pre, -87.0) * -1.4426950408889634)
                sig = pl.reciprocal(bottom, approx=True)
                sig = sig * (2.0 - bottom * sig)
                weight = pre * sig
                dpre = dweight[part] * (sig + weight * (1.0 - sig))
                if diagonal:
                    causal = (self.row_at + strip * self.sub - self.lane_at) * sign >= 0
                    weight = jnp.where(causal, weight, 0.0)
                    dpre = jnp.where(causal, dpre, 0.0)
                if acc is not None:
                    weights.append(weight.astype(BF16))
                    dpres.append(dpre.astype(BF16))
                if banded is None:
                    continue
                whole = jnp.sum(dpre.reshape(self.sub // 8, 8, self.span), axis=0)
                inner = jnp.sum(jnp.where(near, dpre, 0.0).reshape(self.sub // 8, 8, self.span), axis=0)
                for half in range(2):
                    lanes = slice(half * self.rows, (half + 1) * self.rows)
                    for under, amount in ((0, inner[:, lanes]), (1, (whole - inner)[:, lanes])):
                        level = self.level_of(sign * (gap + strip - half * self.strips), under)
                        self.rab[side, head, jnp.where(banded, level, self.bands)] += amount
            if acc is not None:
                weight = jnp.concatenate(weights, axis=0)
                dpre = jnp.concatenate(dpres, axis=0)
                acc[side, 0, :, cols] += jnp.dot(weight, right_b, preferred_element_type=F32)
                acc[side, 1, :, cols] += jnp.dot(dpre, right_a, preferred_element_type=F32)

    def band_row(self, out_ref, core, scale):
        strip_of = lax.broadcasted_iota(jnp.int32, (self.bands, self.rows), 1) // self.sub
        level = lax.broadcasted_iota(jnp.int32, (self.bands, 128), 0)
        lane = lax.broadcasted_iota(jnp.int32, (self.bands, 128), 1)
        result = jnp.zeros((self.bands, 128), F32)
        for head in range(self.heads):
            step_no = lane - (core * self.heads + head) * self.bands
            inside = (step_no >= 0) & (step_no < self.bands)
            for side in range(2):
                sums = jnp.sum(self.rab[side, head, : self.bands], axis=1)
                for strip in range(self.strips):
                    amount = jnp.sum(jnp.where(strip_of == strip, sums, 0.0), axis=1, keepdims=True)
                    band = level - strip if side == 0 else level + strip
                    result = result + jnp.where(inside & (band >= step_no), amount, 0.0)
        row = jnp.sum(result, axis=0, keepdims=True) * scale
        out_ref[...] = jnp.broadcast_to(row[None], out_ref.shape)


def position(rows):
    index = lax.axis_index("seq")
    chip, core = index // 2, lax.rem(index, 2)
    mine = pl.ds(pl.multiple_of(core * rows, rows), rows)
    others = pl.ds(pl.multiple_of((1 - core) * rows, rows), rows)
    return chip, core, mine, others


def own_kernel(steps_ref, kv_ref, qd_ref, acc, rab, cum, *, blocks_of):
    chip, core, _, _ = position(kv_ref.shape[1] // 2)
    acc[...] = jnp.zeros_like(acc)
    rab[...] = jnp.zeros_like(rab)
    blocks = blocks_of(cum, rab)
    blocks.sum_steps(steps_ref, core)
    kv, qd = lambda n, cols: kv_ref[n, :, cols], lambda n, cols: qd_ref[n, :, cols]
    blocks.run(qd, kv, jnp.int32(0), 0, diagonal=True, acc=acc, banded=True)
    blocks.run(kv, qd, jnp.int32(0), 1, diagonal=True, acc=acc)


def middle_kernel(*refs, rounds, done, key_side, ends, blocks_of, scale):
    count = len(rounds)
    steps_ref, kv_ref, qd_ref, acc_in, rab_in = refs[:5]
    pieces = refs[5 : 5 + count]
    if ends is None:
        acc, rab, stack, copied, cum, plan = refs[5 + count :]
    else:
        acc, band_ref, stack, copied, cum, plan, rab = refs[5 + count :]
    rows = kv_ref.shape[1] // 2
    chip, core, _, _ = position(rows)
    chips = lax.axis_size("seq") // 2
    copies = [
        pltpu.make_async_copy(piece, stack.at[unit], copied.at[unit]) for unit, piece in enumerate(pieces)
    ]
    for copy in copies:
        copy.start()
    acc[...] = acc_in[...]
    rab[...] = rab_in[...]
    blocks = blocks_of(cum, rab)
    blocks.sum_steps(steps_ref, core)
    for unit, one in enumerate(rounds):
        plan[unit, 0] = of_chip(one.origin, chip)
        plan[unit, 1] = of_chip([int(n in key_side.get(unit, ())) for n in range(chips)], chip)
    for copy in copies:
        copy.wait()
    per_chip = 2 * blocks.strips

    def step(unit, unused):
        origin = plan[unit, 0]
        other = lambda n, cols: stack[unit, n, :, cols]
        gap = (chip - origin) * per_chip

        @pl.when(origin < chip)
        def _():
            blocks.run(lambda n, cols: qd_ref[n, :, cols], other, gap, 0, acc=acc, banded=True)

        @pl.when(origin > chip)
        def _():
            wanted = plan[unit, 1] == 1
            blocks.run(lambda n, cols: kv_ref[n, :, cols], other, gap, 1, acc=acc, banded=wanted)

        return unused

    lax.fori_loop(done, count, step, 0)
    if ends is None:
        return

    tables = [[ends.get(n, (0, 0, -1))[part] for n in range(chips)] for part in range(3)]
    queries_at, keys_at, part = [of_chip(table, chip) for table in tables]

    @pl.when(part >= 0)
    def _():
        place = pl.ds(pl.multiple_of(part * rows, rows), rows)
        blocks.run(
            lambda n, cols: stack[queries_at, n, place, cols],
            lambda n, cols: stack[keys_at, n, :, cols],
            (chips - 1) * per_chip + part * blocks.strips,
            0,
            banded=True,
        )

    blocks.band_row(band_ref, core, scale)


def late_kernel(steps_ref, kv_ref, qd_ref, acc_in, *refs, rounds, blocks_of):
    pieces, (acc, cum) = refs[: len(rounds)], refs[len(rounds) :]
    chip, core, _, _ = position(kv_ref.shape[1] // 2)
    acc[...] = acc_in[...]
    blocks = blocks_of(cum, None)
    blocks.sum_steps(steps_ref, core)
    for one, piece in zip(rounds, pieces):
        origin = of_chip(one.origin, chip)
        gap = (chip - origin) * 2 * blocks.strips
        other = lambda n, cols: piece[n, :, cols]

        @pl.when(origin < chip)
        def _():
            blocks.run(lambda n, cols: qd_ref[n, :, cols], other, gap, 0, acc=acc)

        @pl.when(origin > chip)
        def _():
            blocks.run(lambda n, cols: kv_ref[n, :, cols], other, gap, 1, acc=acc)


def results_kernel(len_ref, acc, gate_ref, keep_ref, give_ref, *, scale, inv_root):
    rows = keep_ref.shape[1]
    chip, core, mine, others = position(rows)
    for out_ref, place, whose in ((give_ref, others, 1 - core), (keep_ref, mine, core)):
        start = (2 * chip + whose) * rows
        live = start + lax.broadcasted_iota(jnp.int32, (rows, 1), 0) < len_ref[0]
        attended = jnp.where(live, acc[0, 0, place] * scale, 0.0)
        out_ref[0] = (attended * gate_ref[0, place].astype(F32)).astype(BF16)
        out_ref[1] = (acc[0, 1, place] * (scale * inv_root)).astype(BF16)
        out_ref[2] = (acc[1, 1, place] * (scale * inv_root)).astype(BF16)
        out_ref[3] = (acc[1, 0, place] * scale).astype(BF16)
        out_ref[4] = (attended * gate_ref[1, place].astype(F32)).astype(BF16)


def assemble_kernel(keep_ref, got_ref, *refs):
    outs, (buf, copied) = refs[:5], refs[5:]
    wide = keep_ref.shape[2]
    core = lax.rem(lax.axis_index("seq"), 2)
    for half in range(2):

        @pl.when(core == half)
        def _():
            buf[:, :, half * wide : (half + 1) * wide] = keep_ref[...]
            buf[:, :, (1 - half) * wide : (2 - half) * wide] = got_ref[...]

    copies = [pltpu.make_async_copy(buf.at[n], out.at[0], copied.at[n]) for n, out in enumerate(outs)]
    for copy in copies:
        copy.start()
    for copy in copies:
        copy.wait()


def rab_kernel(rows_ref, rab_ref, *, total_len):
    heads, bands = rab_ref.shape
    row = jnp.sum(rows_ref[...], axis=0)[:1] / total_len
    for head in range(heads):
        rab_ref[head : head + 1, :] = row[:, head * bands : (head + 1) * bands]


def params(**more):
    return dict(
        compiler_params=pltpu.CompilerParams(vmem_limit_bytes=VMEM_LIMIT),
        cost_estimate=pl.CostEstimate(flops=1, bytes_accessed=1, transcendentals=0),
        **more,
    )


def body(queries, keys, values, gates, lengths, rab_steps, out_grad, dp_size, seq_size):
    rows, width = queries.shape[1:]
    heads, bands = rab_steps.shape
    total_len = rows * seq_size
    chips = seq_size // 2
    span, wide, depth = 2 * rows, width // 2, width // heads
    inv_root, scale = depth**-0.5, total_len**-0.5
    blocks_of = functools.partial(
        Blocks, span=span, depth=depth, heads=heads // 2, bands=bands, band_width=total_len // bands, inv_root=inv_root
    )

    def send(value, route):
        pairs = [(2 * n + core, 2 * target + core) for n, target in route.items() for core in range(2)]
        return lax.ppermute(value, "seq", pairs)

    across_chip = [(n, n ^ 1) for n in range(seq_size)]
    packed = jax.ShapeDtypeStruct((6, rows, wide), BF16)
    same, cross = pl.pallas_call(
        prep_kernel,
        out_shape=(packed, packed),
        in_specs=[SMEM] + [HBM] * 5,
        out_specs=(VMEM,) * 2,
        scratch_shapes=[pltpu.VMEM((5, rows, width), BF16), pltpu.SemaphoreType.DMA((5,))],
        compiler_params=pltpu.CompilerParams(vmem_limit_bytes=PREP_LIMIT),
        name="prep",
    )(lengths, keys, values, queries, gates, out_grad)
    own = jax.ShapeDtypeStruct((2, span, wide), BF16)
    own_kv, own_qd, gate, low, even = pl.pallas_call(
        functools.partial(build_kernel, chips=chips),
        out_shape=(own,) * 5,
        in_specs=[VMEM] * 2,
        out_specs=(VMEM,) * 5,
        compiler_params=pltpu.CompilerParams(vmem_limit_bytes=VMEM_LIMIT),
        name="build",
    )(same, lax.ppermute(cross, "seq", across_chip))

    early, late, key_side, ends = plan_rounds(chips)
    ready = {"kv": own_kv, "qd": own_qd, "low": low, "even": even}
    got = [send(ready[one.payload], one.route) if isinstance(one.payload, str) else None for one in early]

    acc = jax.ShapeDtypeStruct((2, 2, span, wide), F32)
    rab = jax.ShapeDtypeStruct((2, heads // 2, bands + 1, 8, rows), F32)
    cum = pltpu.SMEM((heads // 2, bands), F32)
    acc_now, rab_now = pl.pallas_call(
        functools.partial(own_kernel, blocks_of=blocks_of),
        out_shape=(acc, rab),
        in_specs=[SMEM, VMEM, VMEM],
        out_specs=(VMEM,) * 2,
        scratch_shapes=[cum],
        **params(name="attend_own"),
    )(rab_steps, own_kv, own_qd)

    acc_now, got[0] = lax.optimization_barrier((acc_now, got[0]))
    for n, one in enumerate(early):
        if got[n] is None:
            got[n] = send(got[one.payload], one.route)
    def middle(state, done, upto, ends):
        count = dp_size * seq_size if together else seq_size
        second = rab if ends is None else jax.ShapeDtypeStruct((count, 8, 128), F32)
        scratch = [
            pltpu.VMEM((upto, 2, span, wide), BF16),
            pltpu.SemaphoreType.DMA((upto,)),
            cum,
            pltpu.SMEM((upto, 2), jnp.int32),
        ]
        return pl.pallas_call(
            functools.partial(
                middle_kernel,
                rounds=early[:upto],
                done=done,
                key_side=key_side,
                ends=ends,
                blocks_of=blocks_of,
                scale=scale,
            ),
            out_shape=(acc, second),
            in_specs=[SMEM] + [VMEM] * 4 + [ANY] * upto,
            out_specs=(VMEM,) * 2,
            scratch_shapes=scratch if ends is None else scratch + [pltpu.VMEM(rab.shape, F32)],
            **params(name="attend_next" if ends is None else "attend_middle"),
        )(rab_steps, own_kv, own_qd, *state, *got[:upto])

    together = dp_size * seq_size <= 64
    tail = [send(got[late[0].payload], late[0].route)]
    state = middle((acc_now, rab_now), 0, 1, None)
    state, got[1:] = lax.optimization_barrier((state, got[1:]))
    tail += [send(got[one.payload], one.route) for one in late[1:]]
    acc_now, band = middle(state, 1, len(early), ends)
    band, tail[0] = lax.optimization_barrier((band, tail[0]))
    band = lax.all_to_all(band, ("dp", "seq") if together else "seq", 0, 0)
    acc_now = pl.pallas_call(
        functools.partial(late_kernel, rounds=late, blocks_of=blocks_of),
        out_shape=acc,
        in_specs=[SMEM] + [VMEM] * (3 + len(tail)),
        out_specs=VMEM,
        scratch_shapes=[cum],
        **params(name="attend_late"),
    )(rab_steps, own_kv, own_qd, acc_now, *tail)
    acc_now, band = lax.optimization_barrier((acc_now, band))
    if not together:
        band = lax.psum(jnp.sum(band, axis=0, keepdims=True), "dp")
    half_out = jax.ShapeDtypeStruct((5, rows, wide), BF16)
    keep, give = pl.pallas_call(
        functools.partial(results_kernel, scale=scale, inv_root=inv_root),
        out_shape=(half_out, half_out),
        in_specs=[SMEM, VMEM, VMEM],
        out_specs=(VMEM,) * 2,
        **params(name="results"),
    )(lengths, acc_now, gate)
    theirs = lax.ppermute(give, "seq", across_chip)
    out = jax.ShapeDtypeStruct(queries.shape, BF16)
    outs = pl.pallas_call(
        assemble_kernel,
        out_shape=(out,) * 5,
        in_specs=[VMEM] * 2,
        out_specs=(HBM,) * 5,
        scratch_shapes=[pltpu.VMEM((5, rows, width), BF16), pltpu.SemaphoreType.DMA((5,))],
        **params(name="assemble"),
    )(keep, theirs)
    rab_grad = pl.pallas_call(
        functools.partial(rab_kernel, total_len=total_len),
        out_shape=jax.ShapeDtypeStruct((heads, bands), F32),
        in_specs=[VMEM],
        out_specs=VMEM,
        **params(name="bias_grad"),
    )(band)
    return (*outs, rab_grad)


def solution(mesh):
    rows = P("dp", "seq", None)
    return jax.shard_map(
        functools.partial(body, dp_size=mesh.shape["dp"], seq_size=mesh.shape["seq"]),
        mesh=mesh,
        in_specs=(rows, rows, rows, rows, P("dp"), P(), rows),
        out_specs=(rows, rows, rows, rows, rows, P()),
        check_vma=False,
    )
```

```python
import functools

import jax
import jax.numpy as jnp
from jax import lax
from jax.experimental import pallas as pl
from jax.experimental.pallas import tpu as pltpu
from jax.sharding import PartitionSpec as P

F32 = jnp.float32
BF16 = jnp.bfloat16
VMEM = pl.BlockSpec(memory_space=pltpu.VMEM)
SMEM = pl.BlockSpec(memory_space=pltpu.SMEM)
HBM = pl.BlockSpec(memory_space=pltpu.HBM)
ANY = pl.BlockSpec(memory_space=pl.ANY)
VMEM_LIMIT = 40 * 1024 * 1024
PREP_LIMIT = 60 * 1024 * 1024


def nt_dot(left, right):
    return lax.dot_general(left, right, (((1,), (1,)), ((), ())), preferred_element_type=F32)


class Round:
    def __init__(self, chips, payload, route, earlier=()):
        self.payload, self.route = payload, route
        self.origin = list(range(chips))
        for source, target in route.items():
            self.origin[target] = source if isinstance(payload, str) else earlier[payload].origin[source]


def plan_rounds(chips):
    half = chips // 2
    early, late = [], []

    def add(rounds, payload, route):
        rounds.append(Round(chips, payload, route, early))
        return len(rounds) - 1

    if chips == 4:
        inner = add(early, "low", {1: 2, 2: 1})
        outer = add(early, "low", {0: 1, 3: 2})
        across = add(early, "even", {0: 2, 3: 1, 1: 0, 2: 3})
        add(late, inner, {2: 3, 1: 0})
        add(late, across, {2: 3, 1: 0})
        return early, 2, late, {across: (1,)}, {1: (across, outer, 0), 2: (outer, across, 1)}
    far = add(early, "low", {n: n + half if n < half else n - half for n in range(chips)})
    for hops in range(1, half):
        up = add(early, "kv", {n: n + hops for n in range(chips - hops)})
        down = add(early, "qd", {n: n - hops for n in range(hops, chips)})
    held = far
    for hops in range(half, chips - 1):
        route = {n: n + 1 for n in range(hops, chips - 1)} | {n: n - 1 for n in range(1, chips - hops)}
        held = add(early if hops < chips - 2 else late, held, route)
    return early, 1, late, {}, {half - 1: (far, up, 0), half: (down, far, 1)}


def of_chip(table, chip):
    result = jnp.int32(table[0])
    for n in range(1, len(table)):
        result = jnp.where(chip == n, jnp.int32(table[n]), result)
    return result


def prep_kernel(len_ref, k_ref, v_ref, q_ref, u_ref, og_ref, same_ref, cross_ref, buf, copied):
    copies = [
        pltpu.make_async_copy(source.at[0], buf.at[n], copied.at[n])
        for n, source in enumerate((k_ref, v_ref, q_ref, u_ref, og_ref))
    ]
    for copy in copies:
        copy.start()
    rows, width = buf.shape[1:]
    wide = width // 2
    index = lax.axis_index("seq")
    live = index * rows + lax.broadcasted_iota(jnp.int32, (rows, 1), 0) < len_ref[0]
    for copy in copies:
        copy.wait()
    for half in range(2):
        cols = slice(half * wide, (half + 1) * wide)
        grad = buf[3, :, cols].astype(F32) * buf[4, :, cols].astype(F32)
        grad = jnp.where(live, grad, 0.0).astype(BF16)

        def lay_out(out_ref):
            for n in range(3):
                out_ref[n] = buf[n, :, cols]
            out_ref[3] = grad
            out_ref[4] = buf[3, :, cols]
            out_ref[5] = buf[4, :, cols]

        @pl.when(lax.rem(index, 2) == half)
        def _():
            lay_out(same_ref)

        @pl.when(lax.rem(index, 2) != half)
        def _():
            lay_out(cross_ref)


def build_kernel(same_ref, near_ref, kv_ref, qd_ref, gate_ref, low_ref, even_ref, *, chips):
    chip, _, mine, others = position(same_ref.shape[1])
    for place, source in ((mine, same_ref), (others, near_ref)):
        for n, out_ref in enumerate((kv_ref, qd_ref, gate_ref)):
            out_ref[0, place] = source[2 * n]
            out_ref[1, place] = source[2 * n + 1]

    for out_ref, keys_go in ((low_ref, chip < chips // 2), (even_ref, lax.rem(chip, 2) == 0)):

        @pl.when(keys_go)
        def _():
            out_ref[...] = kv_ref[...]

        @pl.when(jnp.logical_not(keys_go))
        def _():
            out_ref[...] = qd_ref[...]


class Blocks:
    def __init__(self, cum, rab, span, depth, heads, bands, band_width, inv_root):
        self.cum, self.rab, self.span, self.depth, self.heads = cum, rab, span, depth, heads
        self.bands, self.band_width, self.inv_root = bands, band_width, inv_root
        self.rows = span // 2
        self.sub = min(self.rows, band_width)
        self.strips = self.rows // self.sub
        self.row_at = lax.broadcasted_iota(jnp.int32, (self.sub, span), 0)
        self.lane_at = lax.broadcasted_iota(jnp.int32, (self.sub, span), 1)
        self.lane_in = lax.rem(self.lane_at, self.sub)
        self.lane_strip = self.lane_at[:1, : self.rows] // self.sub

    def sum_steps(self, steps_ref, core):
        for head in range(self.heads):
            total = steps_ref[core * self.heads + head, 0]
            self.cum[head, 0] = total
            for level in range(1, self.bands):
                total = total + steps_ref[core * self.heads + head, level]
                self.cum[head, level] = total

    def level_of(self, gap, under):
        return jnp.clip(jnp.maximum(gap * self.sub - under, 0) // self.band_width, 0, self.bands - 1)

    def table(self, head, gap, sign, under):
        table = []
        for half in range(2):
            values = None
            for lane_no in range(self.strips):
                level = self.level_of(sign * (gap - half * self.strips - lane_no), under)
                value = jnp.full((1, self.rows), self.cum[head, level], F32)
                values = value if values is None else jnp.where(self.lane_strip == lane_no, value, values)
            table.append(values)
        return jnp.concatenate(table, axis=1)

    def run(self, left, right, gap, side, diagonal=False, acc=None, banded=None):
        sign = 1 - 2 * side
        near = (self.row_at - self.lane_in) * sign >= 0
        for head in range(self.heads):
            cols = slice(head * self.depth, (head + 1) * self.depth)
            left_a, left_b = left(0, cols), left(1, cols)
            right_a, right_b = right(0, cols), right(1, cols)
            score = nt_dot(left_a, right_a)
            dweight = nt_dot(left_b, right_b)
            weights, dpres = [], []
            for strip in range(score.shape[0] // self.sub):
                part = slice(strip * self.sub, (strip + 1) * self.sub)
                bias = jnp.where(
                    near, self.table(head, gap + strip, sign, 0), self.table(head, gap + strip, sign, 1)
                )
                pre = score[part] * self.inv_root + bias
                bottom = 1.0 + jnp.exp2(jnp.maximum(pre, -87.0) * -1.4426950408889634)
                sig = pl.reciprocal(bottom, approx=True)
                sig = sig * (2.0 - bottom * sig)
                weight = pre * sig
                dpre = dweight[part] * (sig + weight * (1.0 - sig))
                if diagonal:
                    causal = (self.row_at + strip * self.sub - self.lane_at) * sign >= 0
                    weight = jnp.where(causal, weight, 0.0)
                    dpre = jnp.where(causal, dpre, 0.0)
                if acc is not None:
                    weights.append(weight.astype(BF16))
                    dpres.append(dpre.astype(BF16))
                if banded is None:
                    continue
                whole = jnp.sum(dpre.reshape(self.sub // 8, 8, self.span), axis=0)
                inner = jnp.sum(jnp.where(near, dpre, 0.0).reshape(self.sub // 8, 8, self.span), axis=0)
                for half in range(2):
                    lanes = slice(half * self.rows, (half + 1) * self.rows)
                    for under, amount in ((0, inner[:, lanes]), (1, (whole - inner)[:, lanes])):
                        level = self.level_of(sign * (gap + strip - half * self.strips), under)
                        self.rab[side, head, jnp.where(banded, level, self.bands)] += amount
            if acc is not None:
                weight = jnp.concatenate(weights, axis=0)
                dpre = jnp.concatenate(dpres, axis=0)
                acc[side, 0, :, cols] += jnp.dot(weight, right_b, preferred_element_type=F32)
                acc[side, 1, :, cols] += jnp.dot(dpre, right_a, preferred_element_type=F32)

    def band_row(self, out_ref, core, scale):
        strip_of = lax.broadcasted_iota(jnp.int32, (self.bands, self.rows), 1) // self.sub
        level = lax.broadcasted_iota(jnp.int32, (self.bands, 128), 0)
        lane = lax.broadcasted_iota(jnp.int32, (self.bands, 128), 1)
        result = jnp.zeros((self.bands, 128), F32)
        for head in range(self.heads):
            step_no = lane - (core * self.heads + head) * self.bands
            inside = (step_no >= 0) & (step_no < self.bands)
            for side in range(2):
                sums = jnp.sum(self.rab[side, head, : self.bands], axis=1)
                for strip in range(self.strips):
                    amount = jnp.sum(jnp.where(strip_of == strip, sums, 0.0), axis=1, keepdims=True)
                    band = level - strip if side == 0 else level + strip
                    result = result + jnp.where(inside & (band >= step_no), amount, 0.0)
        row = jnp.sum(result, axis=0, keepdims=True) * scale
        out_ref[...] = jnp.broadcast_to(row[None], out_ref.shape)


def position(rows):
    index = lax.axis_index("seq")
    chip, core = index // 2, lax.rem(index, 2)
    mine = pl.ds(pl.multiple_of(core * rows, rows), rows)
    others = pl.ds(pl.multiple_of((1 - core) * rows, rows), rows)
    return chip, core, mine, others


def own_kernel(steps_ref, kv_ref, qd_ref, acc, rab, cum, *, blocks_of):
    chip, core, _, _ = position(kv_ref.shape[1] // 2)
    acc[...] = jnp.zeros_like(acc)
    rab[...] = jnp.zeros_like(rab)
    blocks = blocks_of(cum, rab)
    blocks.sum_steps(steps_ref, core)
    kv, qd = lambda n, cols: kv_ref[n, :, cols], lambda n, cols: qd_ref[n, :, cols]
    blocks.run(qd, kv, jnp.int32(0), 0, diagonal=True, acc=acc, banded=True)
    blocks.run(kv, qd, jnp.int32(0), 1, diagonal=True, acc=acc)


def middle_kernel(*refs, rounds, done, key_side, ends, blocks_of, scale):
    count = len(rounds)
    steps_ref, kv_ref, qd_ref, acc_in, rab_in = refs[:5]
    pieces = refs[5 : 5 + count]
    if ends is None:
        acc, rab, stack, copied, cum, plan = refs[5 + count :]
    else:
        acc, band_ref, stack, copied, cum, plan, rab = refs[5 + count :]
    rows = kv_ref.shape[1] // 2
    chip, core, _, _ = position(rows)
    chips = lax.axis_size("seq") // 2
    copies = [
        pltpu.make_async_copy(piece, stack.at[unit], copied.at[unit]) for unit, piece in enumerate(pieces)
    ]
    for copy in copies:
        copy.start()
    acc[...] = acc_in[...]
    rab[...] = rab_in[...]
    blocks = blocks_of(cum, rab)
    blocks.sum_steps(steps_ref, core)
    for unit, one in enumerate(rounds):
        plan[unit, 0] = of_chip(one.origin, chip)
        plan[unit, 1] = of_chip([int(n in key_side.get(unit, ())) for n in range(chips)], chip)
    for copy in copies:
        copy.wait()
    per_chip = 2 * blocks.strips

    def step(unit, unused):
        origin = plan[unit, 0]
        other = lambda n, cols: stack[unit, n, :, cols]
        gap = (chip - origin) * per_chip

        @pl.when(origin < chip)
        def _():
            blocks.run(lambda n, cols: qd_ref[n, :, cols], other, gap, 0, acc=acc, banded=True)

        @pl.when(origin > chip)
        def _():
            wanted = plan[unit, 1] == 1
            blocks.run(lambda n, cols: kv_ref[n, :, cols], other, gap, 1, acc=acc, banded=wanted)

        return unused

    lax.fori_loop(done, count, step, 0)
    if ends is None:
        return

    tables = [[ends.get(n, (0, 0, -1))[part] for n in range(chips)] for part in range(3)]
    queries_at, keys_at, part = [of_chip(table, chip) for table in tables]

    @pl.when(part >= 0)
    def _():
        place = pl.ds(pl.multiple_of(part * rows, rows), rows)
        blocks.run(
            lambda n, cols: stack[queries_at, n, place, cols],
            lambda n, cols: stack[keys_at, n, :, cols],
            (chips - 1) * per_chip + part * blocks.strips,
            0,
            banded=True,
        )

    blocks.band_row(band_ref, core, scale)


def late_kernel(steps_ref, kv_ref, qd_ref, acc_in, *refs, rounds, blocks_of):
    pieces, (acc, cum) = refs[: len(rounds)], refs[len(rounds) :]
    chip, core, _, _ = position(kv_ref.shape[1] // 2)
    acc[...] = acc_in[...]
    blocks = blocks_of(cum, None)
    blocks.sum_steps(steps_ref, core)
    for one, piece in zip(rounds, pieces):
        origin = of_chip(one.origin, chip)
        gap = (chip - origin) * 2 * blocks.strips
        other = lambda n, cols: piece[n, :, cols]

        @pl.when(origin < chip)
        def _():
            blocks.run(lambda n, cols: qd_ref[n, :, cols], other, gap, 0, acc=acc)

        @pl.when(origin > chip)
        def _():
            blocks.run(lambda n, cols: kv_ref[n, :, cols], other, gap, 1, acc=acc)


def results_kernel(len_ref, acc, gate_ref, keep_ref, give_ref, *, scale, inv_root):
    rows = keep_ref.shape[1]
    chip, core, mine, others = position(rows)
    for out_ref, place, whose in ((give_ref, others, 1 - core), (keep_ref, mine, core)):
        start = (2 * chip + whose) * rows
        live = start + lax.broadcasted_iota(jnp.int32, (rows, 1), 0) < len_ref[0]
        attended = jnp.where(live, acc[0, 0, place] * scale, 0.0)
        out_ref[0] = (attended * gate_ref[0, place].astype(F32)).astype(BF16)
        out_ref[1] = (acc[0, 1, place] * (scale * inv_root)).astype(BF16)
        out_ref[2] = (acc[1, 1, place] * (scale * inv_root)).astype(BF16)
        out_ref[3] = (acc[1, 0, place] * scale).astype(BF16)
        out_ref[4] = (attended * gate_ref[1, place].astype(F32)).astype(BF16)


def assemble_kernel(keep_ref, got_ref, *refs):
    outs, (buf, copied) = refs[:5], refs[5:]
    wide = keep_ref.shape[2]
    core = lax.rem(lax.axis_index("seq"), 2)
    for half in range(2):

        @pl.when(core == half)
        def _():
            buf[:, :, half * wide : (half + 1) * wide] = keep_ref[...]
            buf[:, :, (1 - half) * wide : (2 - half) * wide] = got_ref[...]

    copies = [pltpu.make_async_copy(buf.at[n], out.at[0], copied.at[n]) for n, out in enumerate(outs)]
    for copy in copies:
        copy.start()
    for copy in copies:
        copy.wait()


def rab_kernel(rows_ref, rab_ref, *, total_len):
    heads, bands = rab_ref.shape
    row = jnp.sum(rows_ref[...], axis=0)[:1] / total_len
    for head in range(heads):
        rab_ref[head : head + 1, :] = row[:, head * bands : (head + 1) * bands]


def params(**more):
    return dict(
        compiler_params=pltpu.CompilerParams(vmem_limit_bytes=VMEM_LIMIT),
        cost_estimate=pl.CostEstimate(flops=1, bytes_accessed=1, transcendentals=0),
        **more,
    )


def body(queries, keys, values, gates, lengths, rab_steps, out_grad, dp_size, seq_size):
    rows, width = queries.shape[1:]
    heads, bands = rab_steps.shape
    total_len = rows * seq_size
    chips = seq_size // 2
    span, wide, depth = 2 * rows, width // 2, width // heads
    inv_root, scale = depth**-0.5, total_len**-0.5
    blocks_of = functools.partial(
        Blocks, span=span, depth=depth, heads=heads // 2, bands=bands, band_width=total_len // bands, inv_root=inv_root
    )

    def send(value, route):
        pairs = [(2 * n + core, 2 * target + core) for n, target in route.items() for core in range(2)]
        return lax.ppermute(value, "seq", pairs)

    across_chip = [(n, n ^ 1) for n in range(seq_size)]
    packed = jax.ShapeDtypeStruct((6, rows, wide), BF16)
    same, cross = pl.pallas_call(
        prep_kernel,
        out_shape=(packed, packed),
        in_specs=[SMEM] + [HBM] * 5,
        out_specs=(VMEM,) * 2,
        scratch_shapes=[pltpu.VMEM((5, rows, width), BF16), pltpu.SemaphoreType.DMA((5,))],
        compiler_params=pltpu.CompilerParams(vmem_limit_bytes=PREP_LIMIT),
        name="prep",
    )(lengths, keys, values, queries, gates, out_grad)
    own = jax.ShapeDtypeStruct((2, span, wide), BF16)
    own_kv, own_qd, gate, low, even = pl.pallas_call(
        functools.partial(build_kernel, chips=chips),
        out_shape=(own,) * 5,
        in_specs=[VMEM] * 2,
        out_specs=(VMEM,) * 5,
        compiler_params=pltpu.CompilerParams(vmem_limit_bytes=VMEM_LIMIT),
        name="build",
    )(same, lax.ppermute(cross, "seq", across_chip))

    early, split, late, key_side, ends = plan_rounds(chips)
    ready = {"kv": own_kv, "qd": own_qd, "low": low, "even": even}
    got = [send(ready[one.payload], one.route) if isinstance(one.payload, str) else None for one in early]

    acc = jax.ShapeDtypeStruct((2, 2, span, wide), F32)
    rab = jax.ShapeDtypeStruct((2, heads // 2, bands + 1, 8, rows), F32)
    cum = pltpu.SMEM((heads // 2, bands), F32)
    acc_now, rab_now = pl.pallas_call(
        functools.partial(own_kernel, blocks_of=blocks_of),
        out_shape=(acc, rab),
        in_specs=[SMEM, VMEM, VMEM],
        out_specs=(VMEM,) * 2,
        scratch_shapes=[cum],
        **params(name="attend_own"),
    )(rab_steps, own_kv, own_qd)

    acc_now, got[:split] = lax.optimization_barrier((acc_now, got[:split]))
    for n, one in enumerate(early):
        if got[n] is None:
            got[n] = send(got[one.payload], one.route)

    def middle(state, done, upto, ends):
        count = dp_size * seq_size if together else seq_size
        second = rab if ends is None else jax.ShapeDtypeStruct((count, 8, 128), F32)
        scratch = [
            pltpu.VMEM((upto, 2, span, wide), BF16),
            pltpu.SemaphoreType.DMA((upto,)),
            cum,
            pltpu.SMEM((upto, 2), jnp.int32),
        ]
        return pl.pallas_call(
            functools.partial(
                middle_kernel,
                rounds=early[:upto],
                done=done,
                key_side=key_side,
                ends=ends,
                blocks_of=blocks_of,
                scale=scale,
            ),
            out_shape=(acc, second),
            in_specs=[SMEM] + [VMEM] * 4 + [ANY] * upto,
            out_specs=(VMEM,) * 2,
            scratch_shapes=scratch if ends is None else scratch + [pltpu.VMEM(rab.shape, F32)],
            **params(name="attend_next" if ends is None else "attend_middle"),
        )(rab_steps, own_kv, own_qd, *state, *got[:upto])

    together = dp_size * seq_size <= 64
    tail = [send(got[one.payload], one.route) for one in late if one.payload < split]
    ahead = len(tail)
    state = middle((acc_now, rab_now), 0, split, None)
    state, got[split:] = lax.optimization_barrier((state, got[split:]))
    tail += [send(got[one.payload], one.route) for one in late if one.payload >= split]
    acc_now, band = middle(state, split, len(early), ends)
    band, tail[:ahead] = lax.optimization_barrier((band, tail[:ahead]))
    band = lax.all_to_all(band, ("dp", "seq") if together else "seq", 0, 0)
    acc_now = pl.pallas_call(
        functools.partial(late_kernel, rounds=late, blocks_of=blocks_of),
        out_shape=acc,
        in_specs=[SMEM] + [VMEM] * (3 + len(tail)),
        out_specs=VMEM,
        scratch_shapes=[cum],
        **params(name="attend_late"),
    )(rab_steps, own_kv, own_qd, acc_now, *tail)
    acc_now, band = lax.optimization_barrier((acc_now, band))
    if not together:
        band = lax.psum(jnp.sum(band, axis=0, keepdims=True), "dp")
    half_out = jax.ShapeDtypeStruct((5, rows, wide), BF16)
    keep, give = pl.pallas_call(
        functools.partial(results_kernel, scale=scale, inv_root=inv_root),
        out_shape=(half_out, half_out),
        in_specs=[SMEM, VMEM, VMEM],
        out_specs=(VMEM,) * 2,
        **params(name="results"),
    )(lengths, acc_now, gate)
    theirs = lax.ppermute(give, "seq", across_chip)
    out = jax.ShapeDtypeStruct(queries.shape, BF16)
    outs = pl.pallas_call(
        assemble_kernel,
        out_shape=(out,) * 5,
        in_specs=[VMEM] * 2,
        out_specs=(HBM,) * 5,
        scratch_shapes=[pltpu.VMEM((5, rows, width), BF16), pltpu.SemaphoreType.DMA((5,))],
        **params(name="assemble"),
    )(keep, theirs)
    rab_grad = pl.pallas_call(
        functools.partial(rab_kernel, total_len=total_len),
        out_shape=jax.ShapeDtypeStruct((heads, bands), F32),
        in_specs=[VMEM],
        out_specs=VMEM,
        **params(name="bias_grad"),
    )(band)
    return (*outs, rab_grad)


def solution(mesh):
    rows = P("dp", "seq", None)
    return jax.shard_map(
        functools.partial(body, dp_size=mesh.shape["dp"], seq_size=mesh.shape["seq"]),
        mesh=mesh,
        in_specs=(rows, rows, rows, rows, P("dp"), P(), rows),
        out_specs=(rows, rows, rows, rows, rows, P()),
        check_vma=False,
    )
```
